32 devices in a mesh: depth: 2 (over core), tile: 16 (over z, y, x).
Axes of the slice: x: 2, y: 2, z: 4, core: 2. Of those that a mesh axis runs over, the one named last changes fastest.
Arguments:
- transmission: bfloat16 [2, 2, 2048, 4096], P('depth', None, None, 'tile')
- chirp_taps: float32 [5], replicated, may hold values from -0.06 to 0.06
- probe_field: float32 [2, 256, 256], replicated, may hold values from -6 to 6
- records: bfloat16 [16, 2, 256, 256], P('tile'), may hold values from 0 to 2
- pos_row: int32 [16, 2], P('tile'), may hold values from 0 to 1792
- pos_col: int32 [16, 2], P('tile'), may hold values from 0 to 255
- counts: int32 [16], P('tile'), may hold values from 1 to 2, as said below
Outputs:
- gradient: bfloat16 [2, 2, 2048, 4096], P('depth', None, None, 'tile')
The draws below stay inside these ranges and needn't reach their ends.
Inputs may be any that keep to these rules, and one draw needn't show every extreme that they name: Slots 0 to counts[t] - 1 of tile t are live; some tile has 2.
All inputs are finite; a program needn't handle non-finite values.
Results may differ from the reference program's by a relative error of at most 0.011.
Values may be sent and summed in bfloat16 or wider, within the bound.
A program may use at most 64 MiB of HBM per device.

```python
import math
import jax
import jax.numpy as jnp
from jax import lax

W = 256
REACH = 4
SL = 1
TW = 256
H = 2048
CAP = 2
TILES = 16
SLICES = 2
NX = 4096
N_DEPTH = 2


def draw_transmission(key, part):
    first_key, second_key = jax.random.split(key)
    shape_here = (SLICES, H, NX)
    phase = jax.random.uniform(first_key, shape_here, jnp.float32, -math.pi, math.pi)
    amplitude = jnp.exp(jax.random.uniform(second_key, shape_here, jnp.float32, math.log(0.96), 0.0))
    return jnp.stack([amplitude * jnp.cos(phase), amplitude * jnp.sin(phase)], axis=1).astype(jnp.bfloat16)


def draw_counts(key, part):
    first_key, second_key, third_key = jax.random.split(key, 3)
    rolled = jax.random.randint(first_key, (TILES,), 0, 10)
    extra = jax.random.randint(second_key, (TILES,), 1, CAP + 1)
    values = jnp.where(rolled < 3, extra, 1)
    chosen = jax.random.randint(third_key, (), 0, TILES)
    values = jnp.where(jnp.arange(TILES) == chosen, CAP, values)
    return values.astype(jnp.int32)


def set_ends(values, stream_key, low, largest):
    longest = values.shape.index(max(values.shape))
    spots = []
    for shift in (0, 1):
        where = [jax.random.randint(jax.random.fold_in(stream_key, axis), (), 0, length) for axis, length in enumerate(values.shape)]
        where[longest] = (where[longest] + shift) % values.shape[longest]
        spots.append(tuple(where))
    return values.at[spots[0]].set(low).at[spots[1]].set(largest)


def steps_of(key, extent, cuts, least, top_value):
    gain, own = 1.0, jax.random.fold_in(key, 6)
    for position, parts in cuts:
        heights = jnp.exp(jax.random.uniform(jax.random.fold_in(own, position), (parts,), jnp.float32, least / len(cuts), top_value / len(cuts)))
        gain = gain * jnp.repeat(heights, extent[position] // parts).reshape([-1 if axis == position else 1 for axis in range(len(extent))])
    return gain


def gaussian(own_key, dims, deviation, limit, kind=jnp.bfloat16):
    return jnp.clip(deviation * jax.random.normal(own_key, dims, jnp.float32), -limit, limit).astype(kind)


def setup_inputs(seed: int = 0) -> dict:
    splits = jax.random.split(jax.random.key(seed), 8)
    return {
        "transmission": draw_transmission(jax.random.fold_in(splits[7], 71), 0),
        "chirp_taps": jnp.clip(jax.random.uniform(splits[1], (REACH + 1,), jnp.float32, -0.06, 0.06), -0.06, 0.06),
        "probe_field": gaussian(splits[2], (2, W, W), 1.0, 6.0, jnp.float32),
        "records": jnp.clip(2.0 * jax.random.uniform(splits[3], (TILES, CAP, W, W), jnp.float32) ** steps_of(splits[3], (TILES, CAP, W, W), ((0, 16),), -0.2, 0.2), 0.0, 2.0).astype(jnp.bfloat16),
        "pos_row": set_ends(jax.random.randint(splits[4], (TILES, CAP), 0, H - W + 1), jax.random.fold_in(splits[4], 1), 0, H - W).astype(jnp.int32),
        "pos_col": set_ends(jax.random.randint(splits[5], (TILES, CAP), 0, TW), jax.random.fold_in(splits[5], 1), 0, TW - 1).astype(jnp.int32),
        "counts": draw_counts(jax.random.fold_in(splits[7], 71), 0),
    }


def spread_taps(values, chirp_taps, axis_pos):
    reach = chirp_taps.shape[0] - 1
    length = values.shape[axis_pos]
    widths = [(0, 0)] * values.ndim
    widths[axis_pos] = (reach, reach)
    padded = jnp.pad(values, widths)
    total = chirp_taps[0] * values
    for offset in range(1, reach + 1):
        upper = lax.slice_in_dim(padded, reach + offset, reach + offset + length, axis=axis_pos)
        lower = lax.slice_in_dim(padded, reach - offset, reach - offset + length, axis=axis_pos)
        total = total + chirp_taps[offset] * (upper + lower)
    return total

def propagate(wavefield, chirp_taps, sign_value):
    for axis_neg in (-1, -2):
        real_part = wavefield[..., 0, :, :]
        imag_part = wavefield[..., 1, :, :]
        axis_pos = real_part.ndim + axis_neg
        new_real = real_part - sign_value * spread_taps(imag_part, chirp_taps, axis_pos)
        new_imag = imag_part + sign_value * spread_taps(real_part, chirp_taps, axis_pos)
        wavefield = jnp.stack([new_real, new_imag], axis=-3)
    return wavefield

def complex_mul(first, second):
    ar, ai = (first[..., 0, :, :], first[..., 1, :, :])
    br, bi = (second[..., 0, :, :], second[..., 1, :, :])
    return jnp.stack([ar * br - ai * bi, ar * bi + ai * br], axis=-3)

def conj_mul(first, second):
    ar, ai = (first[..., 0, :, :], first[..., 1, :, :])
    br, bi = (second[..., 0, :, :], second[..., 1, :, :])
    return jnp.stack([ar * br + ai * bi, ar * bi - ai * br], axis=-3)

def group_forward(wavefield, windows, chirp_taps):
    incoming = []
    for number in range(windows.shape[1]):
        incoming.append(wavefield)
        wavefield = propagate(complex_mul(windows[:, number], wavefield), chirp_taps, 1.0)
    return (wavefield, jnp.stack(incoming, axis=1))

def group_adjoint(adjoint, windows, incoming, chirp_taps):
    terms = [None] * windows.shape[1]
    for number in reversed(range(windows.shape[1])):
        pulled = propagate(adjoint, chirp_taps, -1.0)
        terms[number] = conj_mul(incoming[:, number], pulled)
        adjoint = conj_mul(windows[:, number], pulled)
    return (adjoint, jnp.stack(terms, axis=1))

def dft_tables(length):
    indices = jnp.arange(length, dtype=jnp.int32)
    product = indices[:, None] * indices[None, :] % length
    angle = product.astype(jnp.float32) * (2.0 * math.pi / length)
    factor = 1.0 / math.sqrt(length)
    return ((jnp.cos(angle) * factor).astype(jnp.bfloat16), (jnp.sin(angle) * factor).astype(jnp.bfloat16))

def left_mul(matrix, values):
    return jnp.einsum('jk,bkl->bjl', matrix.astype(jnp.float32), values.astype(jnp.float32))

def right_mul(values, matrix):
    return jnp.einsum('bjk,kl->bjl', values.astype(jnp.float32), matrix.astype(jnp.float32))

def far_field(exit_wave, intensity, live_mask):
    cos_table, sin_table = dft_tables(exit_wave.shape[-1])
    exit_real = exit_wave[:, 0].astype(jnp.bfloat16)
    exit_imag = exit_wave[:, 1].astype(jnp.bfloat16)
    half_real = (left_mul(cos_table, exit_real) + left_mul(sin_table, exit_imag)).astype(jnp.bfloat16)
    half_imag = (left_mul(cos_table, exit_imag) - left_mul(sin_table, exit_real)).astype(jnp.bfloat16)
    far_real = right_mul(half_real, cos_table) + right_mul(half_imag, sin_table)
    far_imag = right_mul(half_imag, cos_table) - right_mul(half_real, sin_table)
    misfit = (far_real * far_real + far_imag * far_imag - intensity.astype(jnp.float32)) * live_mask[:, None, None]
    grad_real = (misfit * far_real).astype(jnp.bfloat16)
    grad_imag = (misfit * far_imag).astype(jnp.bfloat16)
    back_real = (left_mul(cos_table, grad_real) - left_mul(sin_table, grad_imag)).astype(jnp.bfloat16)
    back_imag = (left_mul(cos_table, grad_imag) + left_mul(sin_table, grad_real)).astype(jnp.bfloat16)
    adj_real = right_mul(back_real, cos_table) - right_mul(back_imag, sin_table)
    adj_imag = right_mul(back_imag, cos_table) + right_mul(back_real, sin_table)
    return jnp.stack([adj_real, adj_imag], axis=1)

def reference(transmission, chirp_taps, probe_field, records, pos_row, pos_col, counts):
    total_cols = transmission.shape[3]
    zero_index = jnp.int32(0)

    def tile_work(tile_id):
        columns = (tile_id * TW + jnp.arange(2 * TW, dtype=jnp.int32)) % total_cols
        extended = jnp.take(transmission, columns, axis=3)
        rows_here = pos_row[tile_id].astype(jnp.int32)
        cols_here = pos_col[tile_id].astype(jnp.int32)

        def window_at(row_start, col_start):
            return lax.dynamic_slice(extended, (zero_index, zero_index, row_start.astype(jnp.int32), col_start.astype(jnp.int32)), (SLICES, 2, W, W))
        windows = jax.vmap(window_at)(rows_here, cols_here).astype(jnp.float32)
        live_mask = (jnp.arange(CAP, dtype=jnp.int32) < counts[tile_id]).astype(jnp.float32)
        wavefield = jnp.broadcast_to(probe_field, (CAP, 2, W, W))
        stored = []
        for group in range(N_DEPTH):
            if group > 0:
                wavefield = lax.optimization_barrier(wavefield.astype(jnp.bfloat16)).astype(jnp.float32)
            wavefield, incoming = group_forward(wavefield, windows[:, group * SL:(group + 1) * SL], chirp_taps)
            stored.append(incoming)
        adjoint = far_field(wavefield, records[tile_id], live_mask)
        pieces = [None] * N_DEPTH
        for group in reversed(range(N_DEPTH)):
            if group < N_DEPTH - 1:
                adjoint = lax.optimization_barrier(adjoint.astype(jnp.bfloat16)).astype(jnp.float32)
            adjoint, pieces[group] = group_adjoint(adjoint, windows[:, group * SL:(group + 1) * SL], stored[group], chirp_taps)
        terms = jnp.concatenate(pieces, axis=1)
        accum = jnp.zeros((SLICES, 2, H, 2 * TW), jnp.float32)
        for slot in range(CAP):
            corner = (zero_index, zero_index, rows_here[slot].astype(jnp.int32), cols_here[slot].astype(jnp.int32))
            current = lax.dynamic_slice(accum, corner, (SLICES, 2, W, W))
            accum = lax.dynamic_update_slice(accum, current + terms[slot], corner)
        return accum
    last_accum = tile_work(jnp.int32(TILES - 1))

    def scan_step(carried, tile_id):
        accum = tile_work(tile_id)
        result = (accum[..., :TW] + carried).astype(jnp.bfloat16)
        return (accum[..., TW:], result)
    unused, tiles_out = lax.scan(scan_step, last_accum[..., TW:], jnp.arange(TILES, dtype=jnp.int32))
    return jnp.moveaxis(tiles_out, 0, 3).reshape(SLICES, 2, H, TILES * TW)
```

```python
import functools
import math

import jax
import jax.numpy as jnp
import numpy as np
from jax import lax
from jax.experimental import pallas as pl
from jax.experimental.pallas import tpu as pltpu
from jax.sharding import PartitionSpec as P

MESH = pl.DeviceIdType.MESH
BF = jnp.bfloat16
F32 = jnp.float32
ALIGN = 16


def dft_tables(length):
    indices = np.arange(length)
    angle = (indices[:, None] * indices[None, :] % length) * (2.0 * math.pi / length)
    factor = 1.0 / math.sqrt(length)
    tables = np.stack([np.cos(angle) * factor, np.sin(angle) * factor])
    return tables.astype(np.float32).astype(jnp.bfloat16)


def dot(first, second):
    return jnp.dot(first, second, preferred_element_type=F32)


def iota(shape, axis):
    return lax.broadcasted_iota(jnp.int32, shape, axis)


def one_hot(shape, offset):
    return jnp.where(iota(shape, 1) == iota(shape, 0) + offset, 1.0, 0.0).astype(BF)


def one_hot_t(shape, offset):
    return jnp.where(iota(shape, 0) == iota(shape, 1) + offset, 1.0, 0.0).astype(BF)


def aligned_start(row, side, height):
    start = jnp.minimum(row // ALIGN * ALIGN, height - side - ALIGN)
    return pl.multiple_of(start, ALIGN)


def propagate(re, im, taps, sign):
    new_re = re - sign * dot(im.astype(BF), taps)
    new_im = im + sign * dot(re.astype(BF), taps)
    out_re = new_re - sign * dot(taps, new_im.astype(BF))
    out_im = new_im + sign * dot(taps, new_re.astype(BF))
    return out_re, out_im


def main_kernel(
    n_tiles,
    rows_ref, cols_ref, counts_ref, taps_ref, rows_any, tr_any, probe_ref, rec_ref, tab_ref,
    left_out, right_out, nrows_out,
    trv, nrows, own_send, own_keep, own_recv, nb_send, nb_recv, lterm, rterm,
    load_sem, pos_send, pos_recv, own_s, own_r, nb_s, nb_r, lt_s, lt_r, rt_s, rt_r, keep_sem,
):
    d = lax.axis_index("depth")
    t = lax.axis_index("tile")
    other = 1 - d
    right = lax.rem(t + 1, n_tiles)
    left = lax.rem(t + n_tiles - 1, n_tiles)
    height = trv.shape[1]
    side = probe_ref.shape[-1]

    load = pltpu.make_async_copy(tr_any, trv, load_sem)
    load.start()

    barrier = pltpu.get_barrier_semaphore()
    for who in ((0, left), (1, left), (0, right), (1, right), (other, t)):
        pl.semaphore_signal(barrier, inc=1, device_id=who, device_id_type=MESH)
    pl.semaphore_wait(barrier, 5)

    pos_copy = pltpu.make_async_remote_copy(
        src_ref=rows_any, dst_ref=nrows, send_sem=pos_send, recv_sem=pos_recv,
        device_id=(d, right), device_id_type=MESH,
    )
    pos_copy.start()

    def rows_at(row, plane):
        block = lax.shift_right_logical(row, side.bit_length() - 1)
        last = height // side - 1
        low = trv[plane, :side, :]
        high = trv[plane, side : 2 * side, :]
        for b in range(1, last + 1):
            after = min(b + 1, last)
            low = jnp.where(block == b, trv[plane, b * side : (b + 1) * side, :], low)
            high = jnp.where(block == b, trv[plane, after * side : (after + 1) * side, :], high)
        shift = row - block * side
        picked = dot(one_hot((side, side), shift), low)
        picked += dot(one_hot((side, side), shift - side), high)
        return picked.astype(BF)

    load.wait()
    row_other = jnp.where(d == 0, rows_ref[0, 1], rows_ref[0, 0])
    row_mine = jnp.where(d == 0, rows_ref[0, 0], rows_ref[0, 1])
    col = jnp.where(d == 0, cols_ref[0, 0], cols_ref[0, 1])
    pos_copy.wait()

    nb_copies = []
    for slot in range(2):
        for plane in range(2):
            nb_send[slot, plane] = rows_at(nrows[0, slot], plane)
        copy = pltpu.make_async_remote_copy(
            src_ref=nb_send.at[slot], dst_ref=nb_recv.at[d],
            send_sem=nb_s.at[slot], recv_sem=nb_r.at[d],
            device_id=(slot, left), device_id_type=MESH,
        )
        copy.start()
        nb_copies.append(copy)
    for plane in range(2):
        own_send[plane] = rows_at(row_other, plane)
    own_copy = pltpu.make_async_remote_copy(
        src_ref=own_send, dst_ref=own_recv, send_sem=own_s, recv_sem=own_r,
        device_id=(other, t), device_id_type=MESH,
    )
    own_copy.start()
    for plane in range(2):
        own_keep[plane] = rows_at(row_mine, plane)
    for slot in range(2):
        nrows_out[0, slot] = nrows[0, slot]

    distance = jnp.abs(iota((side, side), 0) - iota((side, side), 1))
    taps = jnp.zeros((side, side), F32)
    for k in range(taps_ref.shape[0]):
        taps = jnp.where(distance == k, taps_ref[k], taps)
    taps = taps.astype(BF)
    pick_l = one_hot_t((side, side), col)
    pick_r = one_hot_t((side, side), col - side)
    cos, sin = tab_ref[0], tab_ref[1]
    own_copy.wait()

    def window(s):
        pltpu.make_async_remote_copy(
            src_ref=nb_send.at[s], dst_ref=nb_recv.at[s],
            send_sem=nb_s.at[s], recv_sem=nb_r.at[s],
            device_id=(d, left), device_id_type=MESH,
        ).wait_recv()
        mine = jnp.where(d == s, 1.0, 0.0).astype(BF)
        theirs = jnp.where(d == s, 0.0, 1.0).astype(BF)
        parts = []
        for plane in range(2):
            own = own_keep[plane] * mine + own_recv[plane] * theirs
            parts.append(dot(own, pick_l) + dot(nb_recv[s, plane], pick_r))
        return parts

    p_re, p_im = probe_ref[0], probe_ref[1]
    a_re, a_im = window(0)
    u_re, u_im = propagate(a_re * p_re - a_im * p_im, a_re * p_im + a_im * p_re, taps, 1.0)
    u_re, u_im = u_re.astype(BF).astype(F32), u_im.astype(BF).astype(F32)
    b_re, b_im = window(1)
    e_re, e_im = propagate(b_re * u_re - b_im * u_im, b_re * u_im + b_im * u_re, taps, 1.0)
    e_re, e_im = e_re.astype(BF), e_im.astype(BF)
    h_re = (dot(cos, e_re) + dot(sin, e_im)).astype(BF)
    h_im = (dot(cos, e_im) - dot(sin, e_re)).astype(BF)
    f_re = dot(h_re, cos) + dot(h_im, sin)
    f_im = dot(h_im, cos) - dot(h_re, sin)
    live = jnp.where(d < counts_ref[0], 1.0, 0.0)
    misfit = (f_re * f_re + f_im * f_im - rec_ref[d].astype(F32)) * live
    g_re = (misfit * f_re).astype(BF)
    g_im = (misfit * f_im).astype(BF)
    k_re = (dot(cos, g_re) - dot(sin, g_im)).astype(BF)
    k_im = (dot(cos, g_im) + dot(sin, g_re)).astype(BF)
    x_re = dot(k_re, cos) - dot(k_im, sin)
    x_im = dot(k_im, cos) + dot(k_re, sin)

    put_l = one_hot((side, side), col)
    put_r = one_hot((side, side), col - side)
    right_copies = []

    def leave(s, re, im):
        for plane, part in enumerate((re.astype(BF), im.astype(BF))):
            rterm[s, plane] = dot(part, put_r).astype(BF)
        copy = pltpu.make_async_remote_copy(
            src_ref=rterm.at[s], dst_ref=right_out.at[d],
            send_sem=rt_s.at[s], recv_sem=rt_r.at[d],
            device_id=(s, right), device_id_type=MESH,
        )
        copy.start()
        right_copies.append(copy)
        for plane, part in enumerate((re.astype(BF), im.astype(BF))):
            lterm[s, plane] = dot(part, put_l).astype(BF)

    q_re, q_im = propagate(x_re, x_im, taps, -1.0)
    leave(1, u_re * q_re + u_im * q_im, u_re * q_im - u_im * q_re)
    y_re = (b_re * q_re + b_im * q_im).astype(BF).astype(F32)
    y_im = (b_re * q_im - b_im * q_re).astype(BF).astype(F32)
    q_re, q_im = propagate(y_re, y_im, taps, -1.0)
    leave(0, p_re * q_re + p_im * q_im, p_re * q_im - p_im * q_re)

    left_copy = pltpu.make_async_remote_copy(
        src_ref=lterm.at[other], dst_ref=left_out.at[d],
        send_sem=lt_s, recv_sem=lt_r,
        device_id=(other, t), device_id_type=MESH,
    )
    left_copy.start()
    keep = pltpu.make_async_copy(lterm.at[d], left_out.at[d], keep_sem)
    keep.start()
    keep.wait()
    left_copy.wait_send()
    pltpu.make_async_remote_copy(
        src_ref=lterm.at[other], dst_ref=left_out.at[other],
        send_sem=lt_s, recv_sem=lt_r,
        device_id=(other, t), device_id_type=MESH,
    ).wait_recv()
    for copy in nb_copies + right_copies:
        copy.wait_send()
    for slot in range(2):
        pltpu.make_async_remote_copy(
            src_ref=rterm.at[slot], dst_ref=right_out.at[slot],
            send_sem=rt_s.at[slot], recv_sem=rt_r.at[slot],
            device_id=(d, right), device_id_type=MESH,
        ).wait_recv()


def place_kernel(rows_ref, nrows_ref, left_ref, right_ref, out_ref, acc):
    height = out_ref.shape[1]
    side = left_ref.shape[2]
    acc[...] = jnp.zeros_like(acc)
    for blocks, rows in ((left_ref, rows_ref), (right_ref, nrows_ref)):
        for slot in range(2):
            row = rows[0, slot]
            start = aligned_start(row, side, height)
            spread = one_hot_t((side + ALIGN, side), row - start)
            for plane in range(2):
                acc[plane, pl.ds(start, side + ALIGN), :] += dot(spread, blocks[slot, plane])
    out_ref[...] = acc[...].astype(out_ref.dtype)


def on_device(transmission, chirp_taps, probe_field, records, pos_row, pos_col, counts):
    n_tiles = lax.axis_size("tile")
    side = probe_field.shape[-1]
    height, tile_cols = transmission.shape[2:]
    tables = jnp.asarray(dft_tables(side))
    vmem = pl.BlockSpec(memory_space=pltpu.VMEM)
    smem = pl.BlockSpec(memory_space=pltpu.SMEM)
    anywhere = pl.BlockSpec(memory_space=pl.ANY)
    pair = (2, 2, side, side)
    block = (2, side, side)
    dma = pltpu.SemaphoreType.DMA
    left_terms, right_terms, nrows = pl.pallas_call(
        functools.partial(main_kernel, n_tiles),
        out_shape=[
            jax.ShapeDtypeStruct(pair, BF),
            jax.ShapeDtypeStruct(pair, BF),
            jax.ShapeDtypeStruct((1, 2), jnp.int32),
        ],
        in_specs=[smem, smem, smem, smem, anywhere, anywhere, vmem, vmem, vmem],
        out_specs=[anywhere, anywhere, smem],
        scratch_shapes=[
            pltpu.VMEM((2, height, tile_cols), BF),
            pltpu.SMEM((1, 2), jnp.int32),
            pltpu.VMEM(block, BF), pltpu.VMEM(block, BF), pltpu.VMEM(block, BF),
            pltpu.VMEM(pair, BF), pltpu.VMEM(pair, BF),
            pltpu.VMEM(pair, BF), pltpu.VMEM(pair, BF),
            dma, dma, dma, dma, dma, dma((2,)), dma((2,)), dma, dma, dma((2,)), dma((2,)), dma,
        ],
        compiler_params=pltpu.CompilerParams(
            collective_id=0, has_side_effects=True, vmem_limit_bytes=40 * 1024 * 1024
        ),
        name="ptycho_main",
    )(pos_row, pos_col, counts, chirp_taps, pos_row, transmission[0], probe_field, records[0], tables)
    out = pl.pallas_call(
        place_kernel,
        out_shape=jax.ShapeDtypeStruct((2, height, tile_cols), BF),
        in_specs=[smem, smem, vmem, vmem],
        out_specs=vmem,
        scratch_shapes=[pltpu.VMEM((2, height, tile_cols), F32)],
        compiler_params=pltpu.CompilerParams(vmem_limit_bytes=40 * 1024 * 1024),
        name="ptycho_place",
    )(pos_row, nrows, left_terms, right_terms)
    return out[None]


def solution(mesh):
    in_specs = (
        P("depth", None, None, "tile"),
        P(),
        P(),
        P("tile", None, None, None),
        P("tile", None),
        P("tile", None),
        P("tile"),
    )
    out_specs = P("depth", None, None, "tile")
    return jax.shard_map(
        on_device, mesh=mesh, in_specs=in_specs, out_specs=out_specs, check_vma=False
    )
```
